32 devices in a mesh: row: 8 (over z, y), col: 4 (over x, core).
Axes of the slice: x: 2, y: 2, z: 4, core: 2. Of those that a mesh axis runs over, the one named last changes fastest.
Arguments:
- feats: bfloat16 [16384, 256], P(('row', 'col')), may hold values from -6 to 6
- w_msg: bfloat16 [256, 256], replicated, may hold values from -0.375 to 0.375
- w_self: bfloat16 [256, 256], replicated, may hold values from -0.375 to 0.375
- bias: float32 [256], replicated, may hold values from -3 to 3
- hit_mask: int32 [16384], P(('row', 'col')), may hold values 0 or 1
- block_cols: int32 [8, 4, 48], P('row', 'col'), may hold values from 0 to 31, as said below
- block_count: int32 [8, 4], P('row', 'col'), may hold values from 16 to 48, as said below
- edge_vals: bfloat16 [8, 4, 48, 128, 128], P('row', 'col'), may hold values from -0.1875 to 0.1875
- grad_out: bfloat16 [16384, 256], P(('row', 'col')), may hold values from -3 to 3
Outputs:
- hidden: bfloat16 [16384, 256], P(('row', 'col'))
- grad_feats: bfloat16 [16384, 256], P(('row', 'col'))
- edge_grad: bfloat16 [8, 4, 48, 128, 128], P('row', 'col')
- w_msg_grad: float32 [256, 256], replicated
- w_self_grad: float32 [256, 256], replicated
- bias_grad: float32 [256], replicated
The draws below stay inside these ranges and needn't reach their ends.
Inputs may be any that keep to these rules, and one draw needn't show every extreme that they name: `block_cols`: slot s of a tile serves the tile's local block row s % 16; the block columns of the slots that serve one block row of one tile are different. Slots from block_count on are unused.
All inputs are finite; a program needn't handle non-finite values. No bound on the sum of `hit_mask` on one device may be relied on, other than what follows from the above.
Results may differ from the reference program's by a relative error of at most 0.015.
Values may be sent and summed in bfloat16 or wider, within the bound.
No kernel may reach another device: no remote copies, remote signals or barrier semaphores. Data moves between devices by JAX's collectives and lax.ppermute only.
A program may use at most 128 MiB of HBM per device.

```python
import math
import jax
import jax.numpy as jnp
from jax import lax

F = 256
BLOCK = 128
HB = 4
K = 3
HITS = 16384
CAP = 48
N_ROW = 8
N_COL = 4


def slot_table(key):
    base = jax.random.fold_in(key, 17)
    key_near, key_far, key_count, key_top = jax.random.split(base, 4)
    tile_total = N_ROW * N_COL
    tile_rows = N_COL * HB
    tile_cols = N_ROW * HB
    block_total = HB * N_ROW * N_COL
    tile_index = jnp.arange(tile_total, dtype=jnp.int32)
    tile_row = tile_index // N_COL
    tile_col = tile_index % N_COL
    local_cols = jnp.arange(tile_cols, dtype=jnp.int32)
    global_rows = tile_row[:, None] * tile_rows + jnp.arange(tile_rows, dtype=jnp.int32)[None, :]
    global_cols = (local_cols[None, :] // HB * N_COL + tile_col[:, None]) * HB + local_cols[None, :] % HB
    spread = jnp.abs(global_cols[:, None, :] - global_rows[:, :, None])
    spread = jnp.minimum(spread, block_total - spread)
    near_noise = jax.random.randint(key_near, (tile_total, tile_rows, tile_cols), 0, 1024)
    near_score = jnp.where(spread <= 2 * tile_rows, 2097152, 0) + near_noise * 1024 + local_cols[None, None, :]
    first = lax.top_k(near_score, 1)[1].astype(jnp.int32)
    far_noise = jax.random.randint(key_far, (tile_total, tile_rows, tile_cols), 0, 1024)
    far_score = far_noise * 1024 + local_cols[None, None, :]
    far_score = jnp.where(local_cols[None, None, :] == first, -1, far_score)
    rest = lax.top_k(far_score, K - 1)[1].astype(jnp.int32)
    picks = jnp.concatenate([first, rest], axis=-1)
    slot_cols = jnp.transpose(picks, (0, 2, 1)).reshape(tile_total, CAP)
    slot_counts = jax.random.randint(key_count, (tile_total,), CAP // 3, CAP + 1)
    busiest = jax.random.randint(key_top, (), 0, tile_total)
    slot_counts = jnp.where(tile_index == busiest, CAP, slot_counts)
    slot_counts = jnp.where(tile_index == (busiest + 1) % tile_total, CAP // 3, slot_counts)
    return (slot_cols.astype(jnp.int32), slot_counts.astype(jnp.int32))


def draw_block_cols(key, part):
    slot_cols, slot_counts = slot_table(key)
    return slot_cols.reshape(N_ROW, N_COL, CAP).astype(jnp.int32)


def draw_block_count(key, part):
    slot_cols, slot_counts = slot_table(key)
    return slot_counts.reshape(N_ROW, N_COL).astype(jnp.int32)


def with_ends(values, own_key, least, largest):
    longest = values.shape.index(max(values.shape))
    spots = []
    for shift in (0, 1):
        where = [jax.random.randint(jax.random.fold_in(own_key, axis), (), 0, length) for axis, length in enumerate(values.shape)]
        where[longest] = (where[longest] + shift) % values.shape[longest]
        spots.append(tuple(where))
    return values.at[spots[0]].set(least).at[spots[1]].set(largest)


def level_of(key, extent, shards, low, top_value):
    gain = 1.0
    for position, blocks in shards:
        steps = jax.random.uniform(jax.random.fold_in(jax.random.fold_in(key, 6), position), (blocks,), jnp.float32, low / len(shards), top_value / len(shards))
        gain = gain * jnp.repeat(jnp.exp(steps), extent[position] // blocks).reshape((-1,) + (1,) * (len(extent) - 1 - position))
    return gain


def noise(own_key, shape, scale, reach, cuts=(), kind=jnp.bfloat16):
    level = level_of(own_key, shape, cuts, -0.22, 0.18) if cuts else 1.0
    array = jax.random.normal(own_key, shape, jnp.float32) * scale * level
    return jnp.minimum(jnp.maximum(array, -reach), reach).astype(kind)


def setup_inputs(seed: int = 0) -> dict:
    seeds = jax.random.split(jax.random.key(seed), 10)
    return {
        "feats": noise(seeds[0], (HITS, F), 1.0, 6.0, ((0, 32),)),
        "w_msg": noise(seeds[1], (F, F), F ** -0.5, 0.375),
        "w_self": noise(seeds[2], (F, F), F ** -0.5, 0.375),
        "bias": noise(seeds[3], (F,), 0.5, 3.0, (), jnp.float32),
        "hit_mask": with_ends((jax.random.randint(seeds[4], (HITS,), 0, 4) < 3).astype(jnp.int32), jax.random.fold_in(seeds[4], 1), 0, 1),
        "block_cols": draw_block_cols(jax.random.fold_in(seeds[9], 71), 0),
        "block_count": draw_block_count(jax.random.fold_in(seeds[9], 71), 0),
        "edge_vals": noise(seeds[7], (N_ROW, N_COL, CAP, BLOCK, BLOCK), (2 * K * N_COL * BLOCK // 3) ** -0.5, 0.1875, ((0, 8), (1, 4))),
        "grad_out": noise(seeds[8], (HITS, F), 0.5, 3.0, ((0, 32),)),
    }


def reference(feats, w_msg, w_self, bias, hit_mask, block_cols, block_count, edge_vals, grad_out):
    row_mask = hit_mask.astype(jnp.float32)[:, None]
    messages = (jnp.dot(feats, w_msg, preferred_element_type=jnp.float32) * row_mask).astype(jnp.bfloat16)
    tile_rows = N_COL * HB
    tile_cols = N_ROW * HB
    msg_blocks = messages.reshape(HITS // BLOCK, BLOCK, F)
    slot_index = jnp.arange(CAP, dtype=jnp.int32)

    def tile_data(tile_row, tile_col):
        slot_cols = block_cols[tile_row, tile_col]
        slot_live = (slot_index < block_count[tile_row, tile_col]).astype(jnp.float32)
        edge_live = (edge_vals[tile_row, tile_col].astype(jnp.float32) * slot_live[:, None, None]).reshape(K, tile_rows, BLOCK, BLOCK)
        global_cols = ((slot_cols // HB * N_COL + tile_col) * HB + slot_cols % HB).astype(jnp.int32)
        col_blocks = msg_blocks[global_cols].astype(jnp.float32).reshape(K, tile_rows, BLOCK, F)
        return (slot_cols, slot_live, edge_live, col_blocks)

    def forward_tile(tile_row, tile_col):
        slot_cols, slot_live, edge_live, col_blocks = tile_data(tile_row, tile_col)
        return jnp.einsum('krij,krjf->rif', edge_live, col_blocks)

    def forward_row(tile_row):
        parts = lax.map(lambda tile_col: forward_tile(tile_row, tile_col), jnp.arange(N_COL, dtype=jnp.int32))
        return lax.optimization_barrier(jnp.sum(parts, axis=0))
    summed = lax.map(forward_row, jnp.arange(N_ROW, dtype=jnp.int32)).reshape(HITS, F)
    pre = summed + jnp.dot(feats, w_self, preferred_element_type=jnp.float32) + bias
    sig = jax.nn.sigmoid(pre)
    hidden = (pre * sig * row_mask).astype(jnp.bfloat16)
    deriv = sig * (1.0 + pre * (1.0 - sig))
    grad_pre = (grad_out.astype(jnp.float32) * row_mask * deriv).astype(jnp.bfloat16)
    grad_blocks = grad_pre.reshape(N_ROW, tile_rows, BLOCK, F)

    def backward_tile(tile_row, tile_col):
        slot_cols, slot_live, edge_live, col_blocks = tile_data(tile_row, tile_col)
        row_blocks = grad_blocks[tile_row].astype(jnp.float32)
        backward = jnp.einsum('krij,rif->krjf', edge_live, row_blocks).reshape(CAP, BLOCK, F)
        term = jax.ops.segment_sum(backward, slot_cols, num_segments=tile_cols).astype(jnp.bfloat16)
        edge_grad = (jnp.einsum('rif,krjf->krij', row_blocks, col_blocks).reshape(CAP, BLOCK, BLOCK) * slot_live[:, None, None]).astype(jnp.bfloat16)
        return (term, edge_grad)

    def backward_row(total, tile_row):
        terms, edge_grads = lax.map(lambda tile_col: backward_tile(tile_row, tile_col), jnp.arange(N_COL, dtype=jnp.int32))
        return (total + terms.astype(jnp.float32), edge_grads)
    start = jnp.zeros((N_COL, tile_cols, BLOCK, F), jnp.float32)
    total, edge_grad = lax.scan(backward_row, start, jnp.arange(N_ROW, dtype=jnp.int32))
    grad_sum = jnp.transpose(total.reshape(N_COL, N_ROW, HB, BLOCK, F), (1, 0, 2, 3, 4)).reshape(HITS, F)
    grad_msg = (grad_sum * row_mask).astype(jnp.bfloat16)
    grad_feats = (jnp.dot(grad_msg, w_msg.T, preferred_element_type=jnp.float32) + jnp.dot(grad_pre, w_self.T, preferred_element_type=jnp.float32)).astype(jnp.bfloat16)
    factor = 1.0 / math.sqrt(HITS)
    w_msg_grad = jnp.dot(feats.T, grad_msg, preferred_element_type=jnp.float32) * factor
    w_self_grad = jnp.dot(feats.T, grad_pre, preferred_element_type=jnp.float32) * factor
    bias_grad = lax.optimization_barrier(jnp.sum(grad_pre.astype(jnp.float32), axis=0)) * factor
    return (hidden, grad_feats, edge_grad, w_msg_grad, w_self_grad, bias_grad)
```

```python
import functools
import math

import jax
import jax.numpy as jnp
from jax import lax
from jax.experimental import pallas as pl
from jax.experimental.pallas import tpu as pltpu
from jax.sharding import PartitionSpec as P

BF16 = jnp.bfloat16
F32 = jnp.float32
VMEM = pl.BlockSpec(memory_space=pltpu.VMEM)
SMEM = pl.BlockSpec(memory_space=pltpu.SMEM)
ANY = pl.BlockSpec(memory_space=pl.ANY)


def exchange(value, axis, bit):
    size = lax.axis_size(axis)
    return lax.ppermute(value, axis, [(i, i ^ bit) for i in range(size)])


def bits_of(size):
    assert size & (size - 1) == 0
    return [1 << n for n in range(size.bit_length() - 1)]


def gather_by_offset(own, axis):
    held = {0: own}
    for bit in reversed(bits_of(lax.axis_size(axis))):
        for offset in list(held):
            held[offset | bit] = exchange(held[offset], axis, bit)
    return [held[k] for k in range(lax.axis_size(axis))]


def scatter_by_offset(parts, axis):
    parts = dict(enumerate(parts))
    last = []
    for bit in bits_of(lax.axis_size(axis)):
        for offset in sorted(parts, reverse=True):
            if offset & bit:
                got = exchange(parts.pop(offset), axis, bit)
                if offset ^ bit:
                    base = parts[offset ^ bit].astype(F32)
                    parts[offset ^ bit] = (base + got.astype(F32)).astype(BF16)
                else:
                    last.append(got)
    return [parts[0]] + last


def nbytes(shape, dtype):
    return math.prod(shape) * jnp.dtype(dtype).itemsize


def kernel_call(body, outs, in_specs, out_specs, scratch, flops, args):
    listed = jax.tree.leaves(outs)
    moved = sum(nbytes(a.shape, a.dtype) for a in (*args, *listed))
    return pl.pallas_call(
        body,
        out_shape=outs,
        in_specs=in_specs,
        out_specs=out_specs,
        scratch_shapes=scratch,
        compiler_params=pltpu.CompilerParams(vmem_limit_bytes=56 * 1024 * 1024),
        cost_estimate=pl.CostEstimate(flops=flops, bytes_accessed=moved, transcendentals=0),
    )(*args)


def tn(a, b):
    return lax.dot_general(a, b, (((0,), (0,)), ((), ())), preferred_element_type=F32)


def nt(a, b):
    return lax.dot_general(a, b, (((1,), (1,)), ((), ())), preferred_element_type=F32)


def load_all(refs, held, sems):
    rows = refs[0].shape[0]
    copies = [
        pltpu.make_async_copy(ref, held.at[pl.ds(k * rows, rows)], sems.at[k])
        for k, ref in enumerate(refs)
    ]
    for copy in copies:
        copy.start()
    return copies


def spmm_body(n_row, n_col, size, depth, cols, count, place, edges, *refs):
    held_refs, outs, (held, sems) = refs[:n_row], refs[n_row : n_row + n_col], refs[n_row + n_col :]
    own = outs[0].shape[0] // size
    tile_rows = n_col * own
    for copy in load_all(held_refs, held, sems):
        copy.wait()
    r, c, used = place[0], place[1], count[0]
    for offset in range(n_col):
        for i in range(own):
            row = (c ^ offset) * own + i
            total = None
            for k in range(depth):
                slot = k * tile_rows + row
                m = cols[slot]
                at = ((m // own) ^ r) * own + m % own
                block = edges[slot]
                block = jnp.where(slot < used, block, jnp.zeros_like(block))
                term = jnp.dot(
                    block,
                    held[pl.ds(pl.multiple_of(at * size, size), size), :],
                    preferred_element_type=F32,
                )
                total = term if total is None else total + term
            outs[offset][pl.ds(i * size, size), :] = total.astype(BF16)


def back_body(n_row, n_col, size, depth, cols, count, place, edges, *refs):
    grads, outs = refs[:n_col], refs[n_col : n_col + n_row]
    held, terms, total, sems = refs[n_col + n_row :]
    own = outs[0].shape[0] // size
    tile_rows = n_col * own
    for copy in load_all(grads, held, sems):
        copy.wait()
    r, c, used = place[0], place[1], count[0]
    total[...] = jnp.zeros_like(total)
    for row in range(tile_rows):
        at = ((row // own) ^ c) * own + row % own
        grad = held[pl.ds(pl.multiple_of(at * size, size), size), :]
        for k in range(depth):
            slot = k * tile_rows + row
            terms[slot] = tn(edges[slot], grad)
    for slot in range(depth * tile_rows):
        m = cols[slot]
        at = ((m // own) ^ r) * own + m % own
        spot = pl.ds(pl.multiple_of(at * size, size), size)

        @pl.when(slot < used)
        def _():
            total[spot, :] = total[spot, :] + terms[slot]

    rows = own * size
    for k in range(n_row):
        outs[k][...] = total[pl.ds(k * rows, rows), :].astype(BF16)


def edge_body(n_row, n_col, size, depth, cols, count, place, *refs):
    grads, feats = refs[:n_col], refs[n_col : n_col + n_row]
    out, held, held_feats, sems, feat_sems = refs[n_col + n_row :]
    own = grads[0].shape[0] // size
    tile_rows = n_col * own
    first, second = load_all(grads, held, sems), load_all(feats, held_feats, feat_sems)
    for copy in first + second:
        copy.wait()
    r, c, used = place[0], place[1], count[0]
    for row in range(tile_rows):
        at = ((row // own) ^ c) * own + row % own
        grad = held[pl.ds(pl.multiple_of(at * size, size), size), :]
        for k in range(depth):
            slot = k * tile_rows + row
            m = cols[slot]
            spot = ((m // own) ^ r) * own + m % own
            value = nt(grad, held_feats[pl.ds(pl.multiple_of(spot * size, size), size), :])
            out[slot] = jnp.where(slot < used, value, jnp.zeros_like(value)).astype(BF16)


def act_body(step, n_terms, *refs):
    terms = refs[:n_terms]
    feats, w_msg, w_self, bias, mask, grad_out, hidden, grad_pre, grad_w, summed = refs[n_terms:]
    for at in range(0, feats.shape[0], step):
        rows = pl.ds(at, step)
        total = terms[0][rows, :].astype(F32)
        for term in terms[1:]:
            total = total + term[rows, :].astype(F32)
        high = total.astype(BF16)
        low = (total - high.astype(F32)).astype(BF16)
        summed[rows, :] = high
        pre = jnp.dot(high, w_msg[...], preferred_element_type=F32)
        pre = pre + jnp.dot(low, w_msg[...], preferred_element_type=F32)
        pre = pre + jnp.dot(feats[rows, :], w_self[...], preferred_element_type=F32) + bias[...]
        live = mask[rows, :].astype(F32)
        sig = jax.nn.sigmoid(pre)
        hidden[rows, :] = (pre * sig * live).astype(BF16)
        deriv = sig * (1.0 + pre * (1.0 - sig))
        grad = (grad_out[rows, :].astype(F32) * live * deriv).astype(BF16)
        grad_pre[rows, :] = grad
        grad_w[rows, :] = nt(grad, w_msg[...]).astype(BF16)


def weight_body(n_col, factor, place, summed, feats, grad_pre, w_self, even, odd, own_part, stack):
    width = feats.shape[1]
    grad = grad_pre[...]
    own_part[...] = nt(grad, w_self[...])
    stack[pl.ds(0, width), :] = tn(summed[...], grad) * factor
    stack[pl.ds(width, width), :] = tn(feats[...], grad) * factor
    rest = stack.shape[0] - 2 * width
    total = jnp.sum(grad.astype(F32), axis=0, keepdims=True) * factor
    stack[pl.ds(2 * width, rest), :] = jnp.broadcast_to(total, (rest, width))
    c = place[1]
    piece = stack.shape[0] // n_col
    for k in range(n_col):
        spot = pl.ds(pl.multiple_of((c ^ k) * piece, 8), piece)
        (odd if k % 2 else even)[k // 2] = stack[spot, :]


def join_body(n_col, place, even, odd, w_msg, w_self, bias, stack):
    c = place[1]
    piece = stack.shape[0] // n_col
    width = w_msg.shape[0]
    for k in range(n_col):
        spot = pl.ds(pl.multiple_of((c ^ k) * piece, 8), piece)
        stack[spot, :] = (odd if k % 2 else even)[k // 2]
    w_msg[...] = stack[pl.ds(0, width), :]
    w_self[...] = stack[pl.ds(width, width), :]
    bias[...] = stack[pl.ds(2 * width, 1), :]


def per_device(feats, w_msg, w_self, bias, hit_mask, block_cols, block_count, edge_vals, grad_out):
    n_row, n_col = lax.axis_size("row"), lax.axis_size("col")
    own_rows, width = feats.shape
    edges = edge_vals[0, 0]
    slots, size = edges.shape[0], edges.shape[1]
    own = own_rows // size
    tile_rows = n_col * own
    depth = slots // tile_rows
    cols, count = block_cols[0, 0], block_count[0]
    place = jnp.stack([lax.axis_index("row"), lax.axis_index("col")]).astype(jnp.int32)
    mask = hit_mask[:, None]
    block = jax.ShapeDtypeStruct((own_rows, width), BF16)
    wide = jax.ShapeDtypeStruct((own_rows, width), F32)
    edge_flops = 2 * slots * size * size * width
    dims = (n_row, n_col, size, depth)
    sems = pltpu.SemaphoreType.DMA

    masked = jnp.where(mask != 0, feats, jnp.zeros_like(feats))
    held = gather_by_offset(masked, "row")

    partial = kernel_call(
        functools.partial(spmm_body, *dims),
        [block] * n_col,
        [SMEM] * 3 + [VMEM] + [ANY] * n_row,
        [VMEM] * n_col,
        [pltpu.VMEM((n_row * own_rows, width), BF16), sems((n_row,))],
        edge_flops,
        (cols, count, place, edges, *held),
    )
    terms = scatter_by_offset(partial, "col")

    hidden, grad_pre, grad_w, summed = kernel_call(
        functools.partial(act_body, size, len(terms)),
        [block] * 4,
        [VMEM] * (len(terms) + 6),
        [VMEM] * 4,
        [],
        10 * own_rows * width * width,
        (*terms, feats, w_msg, w_self, bias[None, :], mask, grad_out),
    )
    grads = gather_by_offset(grad_w, "col")

    pieces = kernel_call(
        functools.partial(back_body, *dims),
        [block] * n_row,
        [SMEM] * 3 + [VMEM] + [ANY] * n_col,
        [VMEM] * n_row,
        [
            pltpu.VMEM((n_col * own_rows, width), BF16),
            pltpu.VMEM((slots, size, width), F32),
            pltpu.VMEM((n_row * own_rows, width), F32),
            sems((n_col,)),
        ],
        edge_flops,
        (cols, count, place, edges, *grads),
    )

    rows = 2 * width + 8
    rows += -rows % (8 * n_col)
    half = jax.ShapeDtypeStruct((n_col // 2, rows // n_col, width), F32)
    factor = 1.0 / math.sqrt(own_rows * n_row * n_col)
    even, odd, own_part = kernel_call(
        functools.partial(weight_body, n_col, factor),
        [half, half, wide],
        [SMEM] + [VMEM] * 4,
        [VMEM] * 3,
        [pltpu.VMEM((rows, width), F32)],
        6 * own_rows * width * width,
        (place, summed, feats, grad_pre, w_self),
    )
    part = even + exchange(odd, "col", 1)
    for bit in bits_of(n_col)[1:]:
        part = jnp.stack([part[k] for k in range(0, part.shape[0], 2)]) + exchange(
            jnp.stack([part[k] for k in range(1, part.shape[0], 2)]), "col", bit
        )
    total = part[0]
    for bit in bits_of(n_row):
        total = total + exchange(total, "row", bit)
    found = total[None]
    for bit in reversed(bits_of(n_col)[1:]):
        other = exchange(found, "col", bit)
        found = jnp.stack([found, other], axis=1).reshape(-1, *total.shape)
    other = exchange(found, "col", 1)
    square = jax.ShapeDtypeStruct((width, width), F32)
    msg_grad, self_grad, bias_grad = kernel_call(
        functools.partial(join_body, n_col),
        [square, square, jax.ShapeDtypeStruct((1, width), F32)],
        [SMEM] + [VMEM] * 2,
        [VMEM] * 3,
        [pltpu.VMEM((rows, width), F32)],
        0,
        (place, found, other),
    )

    edge_grad = kernel_call(
        functools.partial(edge_body, *dims),
        jax.ShapeDtypeStruct((slots, size, size), BF16),
        [SMEM] * 3 + [ANY] * (n_col + n_row),
        VMEM,
        [
            pltpu.VMEM((n_col * own_rows, width), BF16),
            pltpu.VMEM((n_row * own_rows, width), BF16),
            sems((n_col,)),
            sems((n_row,)),
        ],
        edge_flops,
        (cols, count, place, *grads, *held),
    )

    back = scatter_by_offset(pieces, "row")
    summed_back = sum(term.astype(F32) for term in back)
    grad_feats = (jnp.where(mask != 0, summed_back, 0.0) + own_part).astype(BF16)
    return hidden, grad_feats, edge_grad[None, None], msg_grad, self_grad, bias_grad[0]


def solution(mesh):
    placed = (
        P(("row", "col"), None),
        P(),
        P(),
        P(),
        P(("row", "col")),
        P("row", "col", None),
        P("row", "col"),
        P("row", "col", None, None, None),
        P(("row", "col"), None),
    )
    return jax.shard_map(
        per_device,
        mesh=mesh,
        in_specs=placed,
        out_specs=(
            P(("row", "col"), None),
            P(("row", "col"), None),
            P("row", "col", None, None, None),
            P(),
            P(),
            P(),
        ),
        check_vma=False,
    )
```

```python
import functools
import math

import jax
import jax.numpy as jnp
from jax import lax
from jax.experimental import pallas as pl
from jax.experimental.pallas import tpu as pltpu
from jax.sharding import PartitionSpec as P

BF16 = jnp.bfloat16
F32 = jnp.float32
VMEM = pl.BlockSpec(memory_space=pltpu.VMEM)
HBM = pl.BlockSpec(memory_space=pltpu.HBM)
SMEM = pl.BlockSpec(memory_space=pltpu.SMEM)


def exchange(value, axis, bit):
    size = lax.axis_size(axis)
    return lax.ppermute(value, axis, [(i, i ^ bit) for i in range(size)])


def bits_of(size):
    assert size & (size - 1) == 0
    return [1 << n for n in range(size.bit_length() - 1)]


def tie(*values):
    return lax.optimization_barrier(values)


def gather_by_offset(own, axis):
    held = {0: own}
    for bit in reversed(bits_of(lax.axis_size(axis))):
        for offset in list(held):
            held[offset | bit] = exchange(held[offset], axis, bit)
    return [held[k] for k in range(lax.axis_size(axis))]


def gather_rows(own, axis):
    size = lax.axis_size(axis)
    if size != 8:
        held = gather_by_offset(own, axis)
        return held, held[1]
    near = exchange(own, axis, 1)
    far = exchange(own, axis, 4)
    diagonal = exchange(own, axis, 3)
    far, near = tie(far, near)
    middle = exchange(own, axis, 2)
    far_near = exchange(far, axis, 1)
    far_middle = exchange(far, axis, 2)
    far_middle, diagonal = tie(far_middle, diagonal)
    last = exchange(far_middle, axis, 1)
    return [own, near, middle, diagonal, far, far_near, far_middle, last], near


def add_rounded(*terms):
    return sum(term.astype(F32) for term in terms).astype(BF16)


def scatter_by_offset(parts, axis):
    parts = dict(enumerate(parts))
    last = []
    for bit in bits_of(lax.axis_size(axis)):
        for offset in sorted(parts, reverse=True):
            if offset & bit:
                got = exchange(parts.pop(offset), axis, bit)
                if offset ^ bit:
                    parts[offset ^ bit] = add_rounded(parts[offset ^ bit], got)
                else:
                    last.append(got)
    return [parts[0]] + last


def scatter_rows(parts, axis):
    if lax.axis_size(axis) != 8:
        return scatter_by_offset(parts, axis)
    got7 = exchange(parts[7], axis, 1)
    got5 = exchange(parts[5], axis, 1)
    got2 = exchange(parts[2], axis, 2)
    got7, part1, part3 = tie(got7, parts[1], parts[3])
    got6 = exchange(add_rounded(parts[6], got7), axis, 2)
    got1 = exchange(part1, axis, 1)
    got3 = exchange(part3, axis, 3)
    got4 = exchange(add_rounded(parts[4], got5, got6), axis, 4)
    return [parts[0], got1, got2, got3, got4]


def nbytes(shape, dtype):
    return math.prod(shape) * jnp.dtype(dtype).itemsize


def kernel_call(body, outs, in_specs, out_specs, scratch, flops, args):
    listed = jax.tree.leaves(outs)
    moved = sum(nbytes(a.shape, a.dtype) for a in (*args, *listed))
    held = moved + sum(nbytes(x.shape, x.dtype) for x in scratch if x.shape[-1] > 8)
    return pl.pallas_call(
        body,
        out_shape=outs,
        in_specs=in_specs,
        out_specs=out_specs,
        scratch_shapes=scratch,
        compiler_params=pltpu.CompilerParams(vmem_limit_bytes=held + held // 4 + 4 * 1024 * 1024),
        cost_estimate=pl.CostEstimate(flops=flops, bytes_accessed=moved, transcendentals=0),
    )(*args)


def tn(a, b):
    return lax.dot_general(a, b, (((0,), (0,)), ((), ())), preferred_element_type=F32)


def nt(a, b):
    return lax.dot_general(a, b, (((1,), (1,)), ((), ())), preferred_element_type=F32)


def each(count, step):
    lax.fori_loop(0, count, lambda i, carry: (step(i), carry)[1], 0)


def copy_all(refs, held, size):
    rows = refs[0].shape[0]
    for k, ref in enumerate(refs):

        def move(i):
            held[pl.ds(pl.multiple_of(k * rows + i * size, size), size), :] = ref[
                pl.ds(pl.multiple_of(i * size, size), size), :
            ]

        each(rows // size, move)


def block_of(cols, slot, own, r, size):
    m = cols[slot]
    return pl.ds(pl.multiple_of((((m // own) ^ r) * own + m % own) * size, size), size)


def live_body(count, edges, out):
    used = count[0]

    def move(slot):
        block = edges[slot]
        out[slot] = jnp.where(slot < used, block, jnp.zeros_like(block))

    each(edges.shape[0], move)


def select_rows(mask, k, size):
    shape = (size, size)
    diagonal = lax.broadcasted_iota(jnp.int32, shape, 0) == lax.broadcasted_iota(jnp.int32, shape, 1)
    live = jnp.broadcast_to(mask[pl.ds(k, 1), :], shape) != 0
    return jnp.where(live & diagonal, 1.0, 0.0).astype(BF16)


def mask_body(size, mask, feats, out, mask_here, feats_here, sems):
    first = pltpu.make_async_copy(mask, mask_here, sems.at[0])
    second = pltpu.make_async_copy(feats, feats_here, sems.at[1])
    first.start()
    second.start()
    first.wait()
    second.wait()
    for k in range(mask.shape[0]):
        rows = pl.ds(k * size, size)
        select = select_rows(mask_here, k, size)
        picked = jnp.dot(select, feats_here[rows, :], preferred_element_type=F32)
        out[rows, :] = picked.astype(BF16)


def prepare_body(size, mask, feats, w_msg, w_self, bias, grad_out, base, grad_live, w_out):
    for k in range(mask.shape[0]):
        rows = pl.ds(k * size, size)
        select = select_rows(mask, k, size)
        own = jnp.dot(feats[rows, :], w_self[...], preferred_element_type=F32)
        base[rows, :] = own + bias[...]
        picked = jnp.dot(select, grad_out[rows, :], preferred_element_type=F32)
        grad_live[rows, :] = picked.astype(BF16)
    w_out[...] = w_msg[...]


def spmm_body(n_row, n_col, size, depth, cols, place, edges, *refs):
    feats, outs, held = refs[:n_row], refs[n_row : n_row + n_col], refs[n_row + n_col]
    own = outs[0].shape[0] // size
    copy_all(feats, held, size)
    r, c = place[0], place[1]
    for offset in reversed(range(n_col)):
        for i in range(own):
            row = (c ^ offset) * own + i
            slots = [k * n_col * own + row for k in range(depth)]
            blocks = jnp.concatenate([edges[slot] for slot in slots], axis=1)
            picked = [held[block_of(cols, slot, own, r, size), :] for slot in slots]
            total = jnp.dot(blocks, jnp.concatenate(picked, axis=0), preferred_element_type=F32)
            outs[offset][pl.ds(i * size, size), :] = total.astype(BF16)


def back_body(n_row, n_col, size, depth, cols, place, edges, *refs):
    grads, outs = refs[:n_col], refs[n_col : n_col + n_row]
    terms, total = refs[n_col + n_row :]
    own = outs[0].shape[0] // size
    r, c = place[0], place[1]

    def clear(i):
        rows = pl.ds(pl.multiple_of(i * size, size), size)
        total[rows, :] = jnp.zeros((size, total.shape[1]), F32)

    each(total.shape[0] // size, clear)
    slots = []
    for offset in range(n_col):
        for i in range(own):
            row = (c ^ offset) * own + i
            grad = grads[offset][pl.ds(i * size, size), :]
            for k in range(depth):
                slot = k * n_col * own + row
                terms[len(slots)] = tn(edges[slot], grad)
                slots.append(slot)
    for at, slot in enumerate(slots):
        spot = block_of(cols, slot, own, r, size)
        total[spot, :] = total[spot, :] + terms[at]
    for k in range(n_row):

        def leave(i):
            rows = pl.ds(pl.multiple_of((k * own + i) * size, size), size)
            outs[k][pl.ds(pl.multiple_of(i * size, size), size), :] = total[rows, :].astype(BF16)

        each(own, leave)


def edge_body(n_row, n_col, size, depth, cols, count, place, *refs):
    grads, (held, out) = refs[:n_col], refs[n_col:]
    own = grads[0].shape[0] // size
    r, c, used = place[0], place[1], count[0]
    for offset in range(n_col):
        for i in range(own):
            row = (c ^ offset) * own + i
            grad = grads[offset][pl.ds(i * size, size), :]
            for k in range(depth):
                slot = k * n_col * own + row
                value = nt(grad, held[block_of(cols, slot, own, r, size), :])
                out[slot] = jnp.where(slot < used, value, jnp.zeros_like(value)).astype(BF16)


def activate(size, k, terms, base, grad_live, w_msg):
    rows = pl.ds(k * size, size)
    total = terms[0][rows, :].astype(F32)
    for term in terms[1:]:
        total = total + term[rows, :].astype(F32)
    high = total.astype(BF16)
    low = (total - high.astype(F32)).astype(BF16)
    pre = jnp.dot(high, w_msg[...], preferred_element_type=F32)
    pre = pre + jnp.dot(low, w_msg[...], preferred_element_type=F32) + base[rows, :]
    sig = jax.nn.sigmoid(pre)
    deriv = sig * (1.0 + pre * (1.0 - sig))
    return high, pre, sig, (grad_live[rows, :].astype(F32) * deriv).astype(BF16)


def act_body(size, n_terms, *refs):
    terms = refs[:n_terms]
    base, grad_live, w_msg, grad_w = refs[n_terms:]
    for k in range(base.shape[0] // size):
        grad = activate(size, k, terms, base, grad_live, w_msg)[3]
        grad_w[pl.ds(k * size, size), :] = nt(grad, w_msg[...]).astype(BF16)


def weight_body(size, n_terms, factor, place, mask, *refs):
    terms = refs[:n_terms]
    base, grad_live, w_msg, feats, w_self, hidden, own_part, same, other = refs[n_terms:-3]
    summed, grad_pre, stack = refs[-3:]
    width = feats.shape[1]
    for k in range(feats.shape[0] // size):
        rows = pl.ds(k * size, size)
        high, pre, sig, grad = activate(size, k, terms, base, grad_live, w_msg)
        summed[rows, :] = high
        grad_pre[rows, :] = grad
        value = (pre * sig).astype(BF16)
        picked = jnp.dot(select_rows(mask, k, size), value, preferred_element_type=F32)
        hidden[rows, :] = picked.astype(BF16)
        own_part[rows, :] = nt(grad, w_self[...])
    grad = grad_pre[...]
    stack[pl.ds(0, width), :] = tn(summed[...], grad) * factor
    stack[pl.ds(width, width), :] = tn(feats[...], grad) * factor
    rest = stack.shape[0] - 2 * width
    total = jnp.sum(grad.astype(F32), axis=0, keepdims=True) * factor
    stack[pl.ds(2 * width, rest), :] = jnp.broadcast_to(total, (rest, width))
    half = stack.shape[0] // 2
    core = place[1] % 2
    same[...] = stack[pl.ds(pl.multiple_of(core * half, 8), half), :]
    other[...] = stack[pl.ds(pl.multiple_of((1 - core) * half, 8), half), :]


def join_body(place, same, other, w_msg, w_self, bias, stack):
    width = w_msg.shape[0]
    half = stack.shape[0] // 2
    core = place[1] % 2
    stack[pl.ds(pl.multiple_of(core * half, 8), half), :] = same[...]
    stack[pl.ds(pl.multiple_of((1 - core) * half, 8), half), :] = other[...]
    w_msg[...] = stack[pl.ds(0, width), :]
    w_self[...] = stack[pl.ds(width, width), :]
    bias[...] = stack[pl.ds(2 * width, 1), :]


def per_device(feats, w_msg, w_self, bias, hit_mask, block_cols, block_count, edge_vals, grad_out):
    n_row, n_col = lax.axis_size("row"), lax.axis_size("col")
    own_rows, width = feats.shape
    edges = edge_vals[0, 0]
    slots, size = edges.shape[0], edges.shape[1]
    own = own_rows // size
    tile_rows = n_col * own
    depth = slots // tile_rows
    cols, count = block_cols[0, 0], block_count[0]
    place = jnp.stack([lax.axis_index("row"), lax.axis_index("col")]).astype(jnp.int32)
    mask = hit_mask.reshape(own, size)
    block = jax.ShapeDtypeStruct((own_rows, width), BF16)
    wide = jax.ShapeDtypeStruct((own_rows, width), F32)
    edge_flops = 2 * slots * size * size * width
    dims = (n_row, n_col, size, depth)

    masked = kernel_call(
        functools.partial(mask_body, size),
        block,
        [HBM] * 2,
        VMEM,
        [
            pltpu.VMEM((own, size), jnp.int32),
            pltpu.VMEM((own_rows, width), BF16),
            pltpu.SemaphoreType.DMA((2,)),
        ],
        2 * own_rows * size * width,
        (mask, feats),
    )
    held, early = gather_rows(masked, "row")
    late_count, late_bias, _ = tie(count, bias, early)
    live = kernel_call(
        live_body,
        jax.ShapeDtypeStruct(edges.shape, BF16),
        [SMEM, VMEM],
        VMEM,
        [],
        0,
        (late_count, edges),
    )
    base, grad_live, w_here = kernel_call(
        functools.partial(prepare_body, size),
        [wide, block, jax.ShapeDtypeStruct(w_msg.shape, BF16)],
        [VMEM] * 6,
        [VMEM] * 3,
        [],
        2 * own_rows * width * (width + size),
        (mask, feats, w_msg, w_self, late_bias[None, :], grad_out),
    )

    *partial, together = kernel_call(
        functools.partial(spmm_body, *dims),
        [block] * n_col + [jax.ShapeDtypeStruct((n_row * own_rows, width), BF16)],
        [SMEM] * 2 + [VMEM] * (1 + n_row),
        [VMEM] * (n_col + 1),
        [],
        edge_flops,
        (cols, place, live, *held),
    )
    terms = scatter_by_offset(partial, "col")

    grad_w = kernel_call(
        functools.partial(act_body, size, len(terms)),
        block,
        [VMEM] * (len(terms) + 3),
        VMEM,
        [],
        6 * own_rows * width * width,
        (*terms, base, grad_live, w_here),
    )
    grads = gather_by_offset(grad_w, "col")

    pieces = kernel_call(
        functools.partial(back_body, *dims),
        [block] * n_row,
        [SMEM] * 2 + [VMEM] * (1 + n_col),
        [VMEM] * n_row,
        [
            pltpu.VMEM((slots, size, width), F32),
            pltpu.VMEM((n_row * own_rows, width), F32),
        ],
        edge_flops,
        (cols, place, live, *grads),
    )

    rows = 2 * width + 32
    half = jax.ShapeDtypeStruct((rows // 2, width), F32)
    factor = 1.0 / math.sqrt(own_rows * n_row * n_col)
    late_live, _ = tie(grad_live, grads[1])
    hidden, own_part, same, other = kernel_call(
        functools.partial(weight_body, size, len(terms), factor),
        [block, wide, half, half],
        [SMEM] + [VMEM] * (len(terms) + 6),
        [VMEM] * 4,
        [
            pltpu.VMEM((own_rows, width), BF16),
            pltpu.VMEM((own_rows, width), BF16),
            pltpu.VMEM((rows, width), F32),
        ],
        14 * own_rows * width * width,
        (place, mask, *terms, base, late_live, w_here, feats, w_self),
    )
    total = same + exchange(other, "col", 1)
    steps = [("row", bit) for bit in reversed(bits_of(n_row))]
    steps = steps[:-1] + [("col", bit) for bit in bits_of(n_col)[1:]] + steps[-1:]
    for axis, bit in steps:
        sent = total.astype(BF16)
        total = sent.astype(F32) + exchange(sent, axis, bit).astype(F32)
    square = jax.ShapeDtypeStruct((width, width), F32)
    msg_grad, self_grad, bias_grad = kernel_call(
        join_body,
        [square, square, jax.ShapeDtypeStruct((1, width), F32)],
        [SMEM] + [VMEM] * 2,
        [VMEM] * 3,
        [pltpu.VMEM((rows, width), F32)],
        0,
        (place, total, exchange(total, "col", 1)),
    )

    edge_grad = kernel_call(
        functools.partial(edge_body, *dims),
        jax.ShapeDtypeStruct((slots, size, size), BF16),
        [SMEM] * 3 + [VMEM] * (n_col + 1),
        VMEM,
        [],
        edge_flops,
        (cols, count, place, *grads, together),
    )

    back = scatter_rows(pieces, "row")
    column = (hit_mask != 0)[:, None]
    early = jnp.where(column, sum(term.astype(F32) for term in back[:-1]), 0.0) + own_part
    early, last = tie(early, back[-1])
    grad_feats = (early + jnp.where(column, last.astype(F32), 0.0)).astype(BF16)
    return hidden, grad_feats, edge_grad[None, None], msg_grad, self_grad, bias_grad[0]


def solution(mesh):
    placed = (
        P(("row", "col"), None),
        P(),
        P(),
        P(),
        P(("row", "col")),
        P("row", "col", None),
        P("row", "col"),
        P("row", "col", None, None, None),
        P(("row", "col"), None),
    )
    return jax.shard_map(
        per_device,
        mesh=mesh,
        in_specs=placed,
        out_specs=(
            P(("row", "col"), None),
            P(("row", "col"), None),
            P("row", "col", None, None, None),
            P(),
            P(),
            P(),
        ),
        check_vma=False,
    )
```

```python
import functools
import math

import jax
import jax.numpy as jnp
from jax import lax
from jax.experimental import pallas as pl
from jax.experimental.pallas import tpu as pltpu
from jax.sharding import PartitionSpec as P

BF16 = jnp.bfloat16
F32 = jnp.float32
VMEM = pl.BlockSpec(memory_space=pltpu.VMEM)
HBM = pl.BlockSpec(memory_space=pltpu.HBM)
SMEM = pl.BlockSpec(memory_space=pltpu.SMEM)


def exchange(value, axis, bit):
    size = lax.axis_size(axis)
    return lax.ppermute(value, axis, [(i, i ^ bit) for i in range(size)])


def bits_of(size):
    assert size & (size - 1) == 0
    return [1 << n for n in range(size.bit_length() - 1)]


def tie(*values):
    return lax.optimization_barrier(values)


def add_over(value, *bits):
    n_row, n_col = lax.axis_size("row"), lax.axis_size("col")
    sent = value.astype(BF16)
    moves = list(bits) if len(bits) == 1 else [*bits, (bits[0][0] ^ bits[1][0], bits[0][1] ^ bits[1][1])]
    got = []
    for row, col in moves:
        pairs = [(i, i ^ (row * n_col + col)) for i in range(n_row * n_col)]
        got.append(lax.ppermute(sent, ("row", "col"), pairs).astype(F32))
    sent = sent.astype(F32)
    return sent + got[0] if len(got) == 1 else (sent + got[0]) + (got[1] + got[2])


def gather_by_offset(own, axis):
    held = {0: own}
    for bit in reversed(bits_of(lax.axis_size(axis))):
        for offset in list(held):
            held[offset | bit] = exchange(held[offset], axis, bit)
    return [held[k] for k in range(lax.axis_size(axis))]


def gather_rows(own, axis):
    size = lax.axis_size(axis)
    if size != 8:
        held = gather_by_offset(own, axis)
        return held, held[1]
    near = exchange(own, axis, 1)
    far = exchange(own, axis, 4)
    diagonal = exchange(own, axis, 3)
    far, near = tie(far, near)
    middle = exchange(own, axis, 2)
    far_near = exchange(far, axis, 1)
    far_middle = exchange(far, axis, 2)
    far_middle, diagonal = tie(far_middle, diagonal)
    last = exchange(far_middle, axis, 1)
    return [own, near, middle, diagonal, far, far_near, far_middle, last], near


def add_rounded(*terms):
    return sum(term.astype(F32) for term in terms).astype(BF16)


def scatter_by_offset(parts, axis):
    parts = dict(enumerate(parts))
    last = []
    for bit in bits_of(lax.axis_size(axis)):
        for offset in sorted(parts, reverse=True):
            if offset & bit:
                got = exchange(parts.pop(offset), axis, bit)
                if offset ^ bit:
                    parts[offset ^ bit] = add_rounded(parts[offset ^ bit], got)
                else:
                    last.append(got)
    return [parts[0]] + last


def scatter_rows(parts, axis):
    if lax.axis_size(axis) != 8:
        return scatter_by_offset(parts, axis)
    got7, got6, got5 = (exchange(parts[4 + bit], axis, bit) for bit in (3, 2, 1))
    got3 = exchange(parts[3], axis, 1)
    far = add_rounded(parts[4], got5, got6, got7)
    got4 = exchange(far, axis, 4)
    _, part1 = tie(far, parts[1])
    got1 = exchange(part1, axis, 1)
    got2 = exchange(add_rounded(parts[2], got3), axis, 2)
    return [parts[0], got1, got2, got4]


def nbytes(shape, dtype):
    return math.prod(shape) * jnp.dtype(dtype).itemsize


def kernel_call(body, outs, in_specs, out_specs, scratch, flops, args):
    listed = jax.tree.leaves(outs)
    moved = sum(nbytes(a.shape, a.dtype) for a in (*args, *listed))
    held = moved + sum(nbytes(x.shape, x.dtype) for x in scratch if x.shape[-1] > 8)
    return pl.pallas_call(
        body,
        out_shape=outs,
        in_specs=in_specs,
        out_specs=out_specs,
        scratch_shapes=scratch,
        compiler_params=pltpu.CompilerParams(vmem_limit_bytes=held + held // 4 + 4 * 1024 * 1024),
        cost_estimate=pl.CostEstimate(flops=flops, bytes_accessed=moved, transcendentals=0),
    )(*args)


def tn(a, b):
    return lax.dot_general(a, b, (((0,), (0,)), ((), ())), preferred_element_type=F32)


def nt(a, b):
    return lax.dot_general(a, b, (((1,), (1,)), ((), ())), preferred_element_type=F32)


def each(count, step):
    lax.fori_loop(0, count, lambda i, carry: (step(i), carry)[1], 0)


def copy_all(refs, held, size):
    rows = refs[0].shape[0]
    for k, ref in enumerate(refs):

        def move(i):
            held[pl.ds(pl.multiple_of(k * rows + i * size, size), size), :] = ref[
                pl.ds(pl.multiple_of(i * size, size), size), :
            ]

        each(rows // size, move)


def block_of(cols, slot, own, r, size):
    m = cols[slot]
    return pl.ds(pl.multiple_of((((m // own) ^ r) * own + m % own) * size, size), size)


def live_body(count, edges, out):
    used = count[0]

    def move(slot):
        block = edges[slot]
        out[slot] = jnp.where(slot < used, block, jnp.zeros_like(block))

    each(edges.shape[0], move)


def select_rows(mask, k, size):
    shape = (size, size)
    diagonal = lax.broadcasted_iota(jnp.int32, shape, 0) == lax.broadcasted_iota(jnp.int32, shape, 1)
    live = jnp.broadcast_to(mask[pl.ds(k, 1), :], shape) != 0
    return jnp.where(live & diagonal, 1.0, 0.0).astype(BF16)


def mask_body(size, mask, feats, out, mask_here, feats_here, sems):
    first = pltpu.make_async_copy(mask, mask_here, sems.at[0])
    second = pltpu.make_async_copy(feats, feats_here, sems.at[1])
    first.start()
    second.start()
    first.wait()
    second.wait()
    for k in range(mask.shape[0]):
        rows = pl.ds(k * size, size)
        select = select_rows(mask_here, k, size)
        picked = jnp.dot(select, feats_here[rows, :], preferred_element_type=F32)
        out[rows, :] = picked.astype(BF16)


def prepare_body(size, mask, feats, w_msg, w_self, bias, grad_out, base, grad_live, w_out, feats_out):
    for k in range(mask.shape[0]):
        rows = pl.ds(k * size, size)
        select = select_rows(mask, k, size)
        own = jnp.dot(feats[rows, :], w_self[...], preferred_element_type=F32)
        base[rows, :] = own + bias[...]
        picked = jnp.dot(select, grad_out[rows, :], preferred_element_type=F32)
        grad_live[rows, :] = picked.astype(BF16)
    w_out[...] = w_msg[...]
    feats_out[...] = feats[...]


def spmm_body(n_row, n_col, size, depth, cols, place, edges, *refs):
    feats, outs, held = refs[:n_row], refs[n_row : n_row + n_col], refs[n_row + n_col]
    own = outs[0].shape[0] // size
    copy_all(feats, held, size)
    r, c = place[0], place[1]
    for offset in reversed(range(n_col)):
        for i in range(own):
            row = (c ^ offset) * own + i
            slots = [k * n_col * own + row for k in range(depth)]
            blocks = jnp.concatenate([edges[slot] for slot in slots], axis=1)
            picked = [held[block_of(cols, slot, own, r, size), :] for slot in slots]
            total = jnp.dot(blocks, jnp.concatenate(picked, axis=0), preferred_element_type=F32)
            outs[offset][pl.ds(i * size, size), :] = total.astype(BF16)


def back_body(n_row, n_col, size, depth, cols, place, edges, *refs):
    grads, outs = refs[:n_col], refs[n_col : n_col + n_row]
    terms, total = refs[n_col + n_row :]
    own = outs[0].shape[0] // size
    r, c = place[0], place[1]

    def clear(i):
        rows = pl.ds(pl.multiple_of(i * size, size), size)
        total[rows, :] = jnp.zeros((size, total.shape[1]), F32)

    each(total.shape[0] // size, clear)
    slots = []
    for offset in range(n_col):
        for i in range(own):
            row = (c ^ offset) * own + i
            grad = grads[offset][pl.ds(i * size, size), :]
            for k in range(depth):
                slot = k * n_col * own + row
                terms[len(slots)] = tn(edges[slot], grad)
                slots.append(slot)
    for at, slot in enumerate(slots):
        spot = block_of(cols, slot, own, r, size)
        total[spot, :] = total[spot, :] + terms[at]
    for k in range(n_row):

        def leave(i):
            rows = pl.ds(pl.multiple_of((k * own + i) * size, size), size)
            outs[k][pl.ds(pl.multiple_of(i * size, size), size), :] = total[rows, :].astype(BF16)

        each(own, leave)


def edge_body(n_row, n_col, size, depth, cols, count, place, *refs):
    grads, (held, out) = refs[:n_col], refs[n_col:]
    own = grads[0].shape[0] // size
    r, c, used = place[0], place[1], count[0]
    for offset in range(n_col):
        for i in range(own):
            row = (c ^ offset) * own + i
            grad = grads[offset][pl.ds(i * size, size), :]
            for k in range(depth):
                slot = k * n_col * own + row
                value = nt(grad, held[block_of(cols, slot, own, r, size), :])
                out[slot] = jnp.where(slot < used, value, jnp.zeros_like(value)).astype(BF16)


def activate(size, k, terms, base, grad_live, w_msg):
    rows = pl.ds(k * size, size)
    total = terms[0][rows, :].astype(F32)
    for term in terms[1:]:
        total = total + term[rows, :].astype(F32)
    high = total.astype(BF16)
    low = (total - high.astype(F32)).astype(BF16)
    pre = jnp.dot(high, w_msg[...], preferred_element_type=F32)
    pre = pre + jnp.dot(low, w_msg[...], preferred_element_type=F32) + base[rows, :]
    sig = jax.nn.sigmoid(pre)
    deriv = sig * (1.0 + pre * (1.0 - sig))
    return high, pre, sig, (grad_live[rows, :].astype(F32) * deriv).astype(BF16)


def act_body(size, n_terms, *refs):
    terms = refs[:n_terms]
    base, grad_live, w_msg, grad_w, grad_pre, summed = refs[n_terms:]
    for k in range(base.shape[0] // size):
        rows = pl.ds(k * size, size)
        high, _, _, grad = activate(size, k, terms, base, grad_live, w_msg)
        summed[rows, :] = high
        grad_pre[rows, :] = grad
        grad_w[rows, :] = nt(grad, w_msg[...]).astype(BF16)


def rest_body(size, n_terms, mask, *refs):
    terms = refs[:n_terms]
    base, grad_live, w_msg, w_self, hidden, own_part = refs[n_terms:]
    for k in range(base.shape[0] // size):
        rows = pl.ds(k * size, size)
        _, pre, sig, grad = activate(size, k, terms, base, grad_live, w_msg)
        value = (pre * sig).astype(BF16)
        picked = jnp.dot(select_rows(mask, k, size), value, preferred_element_type=F32)
        hidden[rows, :] = picked.astype(BF16)
        own_part[rows, :] = nt(grad, w_self[...])


def weight_body(factor, place, feats, grad_pre, summed, same, other, stack):
    width = feats.shape[1]
    grad = grad_pre[...]
    stack[pl.ds(0, width), :] = tn(summed[...], grad) * factor
    stack[pl.ds(width, width), :] = tn(feats[...], grad) * factor
    rest = stack.shape[0] - 2 * width
    total = jnp.sum(grad.astype(F32), axis=0, keepdims=True) * factor
    stack[pl.ds(2 * width, rest), :] = jnp.broadcast_to(total, (rest, width))
    half = stack.shape[0] // 2
    core = place[1] % 2
    same[...] = stack[pl.ds(pl.multiple_of(core * half, 8), half), :]
    other[...] = stack[pl.ds(pl.multiple_of((1 - core) * half, 8), half), :]


def join_body(place, same, other, w_msg, w_self, bias, stack):
    width = w_msg.shape[0]
    half = stack.shape[0] // 2
    core = place[1] % 2
    stack[pl.ds(pl.multiple_of(core * half, 8), half), :] = same[...]
    stack[pl.ds(pl.multiple_of((1 - core) * half, 8), half), :] = other[...]
    w_msg[...] = stack[pl.ds(0, width), :]
    w_self[...] = stack[pl.ds(width, width), :]
    bias[...] = stack[pl.ds(2 * width, 1), :]


def finish_body(size, mask, early, last, out):
    for k in range(mask.shape[0]):
        rows = pl.ds(k * size, size)
        picked = jnp.dot(select_rows(mask, k, size), last[rows, :], preferred_element_type=F32)
        out[rows, :] = (early[rows, :] + picked).astype(BF16)


def per_device(feats, w_msg, w_self, bias, hit_mask, block_cols, block_count, edge_vals, grad_out):
    n_row, n_col = lax.axis_size("row"), lax.axis_size("col")
    own_rows, width = feats.shape
    edges = edge_vals[0, 0]
    slots, size = edges.shape[0], edges.shape[1]
    own = own_rows // size
    tile_rows = n_col * own
    depth = slots // tile_rows
    cols, count = block_cols[0, 0], block_count[0]
    place = jnp.stack([lax.axis_index("row"), lax.axis_index("col")]).astype(jnp.int32)
    mask = hit_mask.reshape(own, size)
    block = jax.ShapeDtypeStruct((own_rows, width), BF16)
    wide = jax.ShapeDtypeStruct((own_rows, width), F32)
    edge_flops = 2 * slots * size * size * width
    dims = (n_row, n_col, size, depth)

    masked = kernel_call(
        functools.partial(mask_body, size),
        block,
        [HBM] * 2,
        VMEM,
        [
            pltpu.VMEM((own, size), jnp.int32),
            pltpu.VMEM((own_rows, width), BF16),
            pltpu.SemaphoreType.DMA((2,)),
        ],
        2 * own_rows * size * width,
        (mask, feats),
    )
    held, early = gather_rows(masked, "row")
    late_count, late_bias, _ = tie(count, bias, early)
    live = kernel_call(
        live_body,
        jax.ShapeDtypeStruct(edges.shape, BF16),
        [SMEM, VMEM],
        VMEM,
        [],
        0,
        (late_count, edges),
    )
    base, grad_live, w_here, feats_here = kernel_call(
        functools.partial(prepare_body, size),
        [wide, block, jax.ShapeDtypeStruct(w_msg.shape, BF16), block],
        [VMEM] * 6,
        [VMEM] * 4,
        [],
        2 * own_rows * width * (width + size),
        (mask, feats, w_msg, w_self, late_bias[None, :], grad_out),
    )

    *partial, together = kernel_call(
        functools.partial(spmm_body, *dims),
        [block] * n_col + [jax.ShapeDtypeStruct((n_row * own_rows, width), BF16)],
        [SMEM] * 2 + [VMEM] * (1 + n_row),
        [VMEM] * (n_col + 1),
        [],
        edge_flops,
        (cols, place, live, *held),
    )
    terms = scatter_by_offset(partial, "col")

    grad_w, grad_pre, summed = kernel_call(
        functools.partial(act_body, size, len(terms)),
        [block] * 3,
        [VMEM] * (len(terms) + 3),
        [VMEM] * 3,
        [],
        6 * own_rows * width * width,
        (*terms, base, grad_live, w_here),
    )
    grads = gather_by_offset(grad_w, "col")

    pieces = kernel_call(
        functools.partial(back_body, *dims),
        [block] * n_row,
        [SMEM] * 2 + [VMEM] * (1 + n_col),
        [VMEM] * n_row,
        [
            pltpu.VMEM((slots, size, width), F32),
            pltpu.VMEM((n_row * own_rows, width), F32),
        ],
        edge_flops,
        (cols, place, live, *grads),
    )

    rows = 2 * width + 32
    half = jax.ShapeDtypeStruct((rows // 2, width), F32)
    factor = 1.0 / math.sqrt(own_rows * n_row * n_col)
    same, other = kernel_call(
        functools.partial(weight_body, factor),
        [half, half],
        [SMEM] + [VMEM] * 3,
        [VMEM] * 2,
        [pltpu.VMEM((rows, width), F32)],
        4 * own_rows * width * width,
        (place, feats_here, grad_pre, summed),
    )
    late_live, _ = tie(grad_live, pieces[0])
    hidden, own_part = kernel_call(
        functools.partial(rest_body, size, len(terms)),
        [block, wide],
        [VMEM] * (len(terms) + 5),
        [VMEM] * 2,
        [],
        8 * own_rows * width * width,
        (mask, *terms, base, late_live, w_here, w_self),
    )
    back = scatter_rows(pieces, "row")
    total = same + exchange(other, "col", 1)
    row_bits, col_bits = bits_of(n_row), bits_of(n_col)[1:]
    total = add_over(total, (row_bits.pop(min(1, len(row_bits) - 1)), 0))
    total, _ = tie(total, pieces[0])
    for bit in reversed(row_bits[1:]):
        total = add_over(total, (bit, 0))
    for bit in col_bits[:-1]:
        total = add_over(total, (0, bit))
    total = add_over(total, (row_bits[0], 0), (0, col_bits[-1]))
    total, *_ = tie(total, *back[2:])
    square = jax.ShapeDtypeStruct((width, width), F32)
    msg_grad, self_grad, bias_grad = kernel_call(
        join_body,
        [square, square, jax.ShapeDtypeStruct((1, width), F32)],
        [SMEM] + [VMEM] * 2,
        [VMEM] * 3,
        [pltpu.VMEM((rows, width), F32)],
        0,
        (place, total, exchange(total, "col", 1)),
    )

    edge_grad = kernel_call(
        functools.partial(edge_body, *dims),
        jax.ShapeDtypeStruct((slots, size, size), BF16),
        [SMEM] * 3 + [VMEM] * (n_col + 1),
        VMEM,
        [],
        edge_flops,
        (cols, count, place, *grads, together),
    )

    column = (hit_mask != 0)[:, None]
    early = jnp.where(column, sum(term.astype(F32) for term in back[:-1]), 0.0) + own_part
    early, last = tie(early, back[-1])
    grad_feats = kernel_call(
        functools.partial(finish_body, size),
        block,
        [VMEM] * 3,
        VMEM,
        [],
        2 * own_rows * size * width,
        (mask, early, last),
    )
    return hidden, grad_feats, edge_grad[None, None], msg_grad, self_grad, bias_grad[0]


def solution(mesh):
    placed = (
        P(("row", "col"), None),
        P(),
        P(),
        P(),
        P(("row", "col")),
        P("row", "col", None),
        P("row", "col"),
        P("row", "col", None, None, None),
        P(("row", "col"), None),
    )
    return jax.shard_map(
        per_device,
        mesh=mesh,
        in_specs=placed,
        out_specs=(
            P(("row", "col"), None),
            P(("row", "col"), None),
            P("row", "col", None, None, None),
            P(),
            P(),
            P(),
        ),
        check_vma=False,
    )
```

```python
import functools
import math

import jax
import jax.numpy as jnp
from jax import lax
from jax.experimental import pallas as pl
from jax.experimental.pallas import tpu as pltpu
from jax.sharding import PartitionSpec as P

BF16 = jnp.bfloat16
F32 = jnp.float32
VMEM = pl.BlockSpec(memory_space=pltpu.VMEM)
HBM = pl.BlockSpec(memory_space=pltpu.HBM)
SMEM = pl.BlockSpec(memory_space=pltpu.SMEM)


def exchange(value, axis, bit):
    size = lax.axis_size(axis)
    return lax.ppermute(value, axis, [(i, i ^ bit) for i in range(size)])


def bits_of(size):
    assert size & (size - 1) == 0
    return [1 << n for n in range(size.bit_length() - 1)]


def tie(*values):
    return lax.optimization_barrier(values)


def add_over(value, *bits):
    n_row, n_col = lax.axis_size("row"), lax.axis_size("col")
    sent = value.astype(BF16)
    moves = list(bits) if len(bits) == 1 else [*bits, (bits[0][0] ^ bits[1][0], bits[0][1] ^ bits[1][1])]
    got = []
    for row, col in moves:
        pairs = [(i, i ^ (row * n_col + col)) for i in range(n_row * n_col)]
        got.append(lax.ppermute(sent, ("row", "col"), pairs).astype(F32))
    sent = sent.astype(F32)
    return sent + got[0] if len(got) == 1 else (sent + got[0]) + (got[1] + got[2])


def gather_by_offset(own, axis):
    held = {0: own}
    for bit in reversed(bits_of(lax.axis_size(axis))):
        for offset in list(held):
            held[offset | bit] = exchange(held[offset], axis, bit)
    return [held[k] for k in range(lax.axis_size(axis))]


def gather_rows(own, axis):
    size = lax.axis_size(axis)
    if size != 8:
        held = gather_by_offset(own, axis)
        return held, held[1]
    near = exchange(own, axis, 1)
    far = exchange(own, axis, 4)
    diagonal = exchange(own, axis, 3)
    far, near = tie(far, near)
    middle = exchange(own, axis, 2)
    far_near = exchange(far, axis, 1)
    far_middle = exchange(far, axis, 2)
    far_middle, diagonal = tie(far_middle, diagonal)
    last = exchange(far_middle, axis, 1)
    return [own, near, middle, diagonal, far, far_near, far_middle, last], near


def add_rounded(*terms):
    return sum(term.astype(F32) for term in terms).astype(BF16)


def scatter_by_offset(parts, axis):
    parts = dict(enumerate(parts))
    last = []
    for bit in bits_of(lax.axis_size(axis)):
        for offset in sorted(parts, reverse=True):
            if offset & bit:
                got = exchange(parts.pop(offset), axis, bit)
                if offset ^ bit:
                    parts[offset ^ bit] = add_rounded(parts[offset ^ bit], got)
                else:
                    last.append(got)
    return [parts[0]] + last


def scatter_rows(parts, axis):
    if lax.axis_size(axis) != 8:
        terms = scatter_by_offset(parts, axis)
        return terms + terms[:1]
    got7, got6, got5 = (exchange(parts[4 + bit], axis, bit) for bit in (3, 2, 1))
    got7, part3 = tie(got7, parts[3])
    got3 = exchange(part3, axis, 1)
    far = add_rounded(parts[4], got5, got6, got7)
    got4 = exchange(far, axis, 4)
    _, part1 = tie(far, parts[1])
    got1 = exchange(part1, axis, 1)
    got2 = exchange(add_rounded(parts[2], got3), axis, 2)
    return [parts[0], got1, got2, got4, far]


def nbytes(shape, dtype):
    return math.prod(shape) * jnp.dtype(dtype).itemsize


def kernel_call(body, outs, in_specs, out_specs, scratch, flops, args):
    listed = jax.tree.leaves(outs)
    moved = sum(nbytes(a.shape, a.dtype) for a in (*args, *listed))
    held = moved + sum(nbytes(x.shape, x.dtype) for x in scratch if x.shape[-1] > 8)
    return pl.pallas_call(
        body,
        out_shape=outs,
        in_specs=in_specs,
        out_specs=out_specs,
        scratch_shapes=scratch,
        compiler_params=pltpu.CompilerParams(vmem_limit_bytes=held + held // 4 + 4 * 1024 * 1024),
        cost_estimate=pl.CostEstimate(flops=flops, bytes_accessed=moved, transcendentals=0),
    )(*args)


def tn(a, b):
    return lax.dot_general(a, b, (((0,), (0,)), ((), ())), preferred_element_type=F32)


def nt(a, b):
    return lax.dot_general(a, b, (((1,), (1,)), ((), ())), preferred_element_type=F32)


def each(count, step):
    lax.fori_loop(0, count, lambda i, carry: (step(i), carry)[1], 0)


def copy_all(refs, held, size):
    rows = refs[0].shape[0]
    for k, ref in enumerate(refs):

        def move(i):
            held[pl.ds(pl.multiple_of(k * rows + i * size, size), size), :] = ref[
                pl.ds(pl.multiple_of(i * size, size), size), :
            ]

        each(rows // size, move)


def block_of(cols, slot, own, r, size):
    m = cols[slot]
    return pl.ds(pl.multiple_of((((m // own) ^ r) * own + m % own) * size, size), size)


def live_body(count, edges, out):
    used = count[0]

    def move(slot):
        block = edges[slot]
        out[slot] = jnp.where(slot < used, block, jnp.zeros_like(block))

    each(edges.shape[0], move)


def select_rows(mask, k, size):
    shape = (size, size)
    diagonal = lax.broadcasted_iota(jnp.int32, shape, 0) == lax.broadcasted_iota(jnp.int32, shape, 1)
    live = jnp.broadcast_to(mask[pl.ds(k, 1), :], shape) != 0
    return jnp.where(live & diagonal, 1.0, 0.0).astype(BF16)


def mask_body(size, mask, feats, out, mask_here, feats_here, sems):
    first = pltpu.make_async_copy(mask, mask_here, sems.at[0])
    second = pltpu.make_async_copy(feats, feats_here, sems.at[1])
    first.start()
    second.start()
    first.wait()
    second.wait()
    for k in range(mask.shape[0]):
        rows = pl.ds(k * size, size)
        select = select_rows(mask_here, k, size)
        picked = jnp.dot(select, feats_here[rows, :], preferred_element_type=F32)
        out[rows, :] = picked.astype(BF16)


def prepare_body(size, mask, feats, w_msg, w_self, bias, grad_out, base, grad_live, w_out, feats_out):
    for k in range(mask.shape[0]):
        rows = pl.ds(k * size, size)
        select = select_rows(mask, k, size)
        own = jnp.dot(feats[rows, :], w_self[...], preferred_element_type=F32)
        base[rows, :] = own + bias[...]
        picked = jnp.dot(select, grad_out[rows, :], preferred_element_type=F32)
        grad_live[rows, :] = picked.astype(BF16)
    w_out[...] = w_msg[...]
    feats_out[...] = feats[...]


def spmm_body(n_row, n_col, size, depth, cols, place, edges, *refs):
    feats, outs, held = refs[:n_row], refs[n_row : n_row + n_col], refs[n_row + n_col]
    own = outs[0].shape[0] // size
    copy_all(feats, held, size)
    r, c = place[0], place[1]
    for offset in reversed(range(n_col)):
        for i in range(own):
            row = (c ^ offset) * own + i
            slots = [k * n_col * own + row for k in range(depth)]
            blocks = jnp.concatenate([edges[slot] for slot in slots], axis=1)
            picked = [held[block_of(cols, slot, own, r, size), :] for slot in slots]
            total = jnp.dot(blocks, jnp.concatenate(picked, axis=0), preferred_element_type=F32)
            outs[offset][pl.ds(i * size, size), :] = total.astype(BF16)


def back_body(n_row, n_col, size, depth, cols, place, edges, *refs):
    grads, outs = refs[:n_col], refs[n_col : n_col + n_row]
    terms, total = refs[n_col + n_row :]
    own = outs[0].shape[0] // size
    r, c = place[0], place[1]

    def clear(i):
        rows = pl.ds(pl.multiple_of(i * size, size), size)
        total[rows, :] = jnp.zeros((size, total.shape[1]), F32)

    each(total.shape[0] // size, clear)
    slots = []
    for offset in range(n_col):
        for i in range(own):
            row = (c ^ offset) * own + i
            grad = grads[offset][pl.ds(i * size, size), :]
            for k in range(depth):
                slot = k * n_col * own + row
                terms[len(slots)] = tn(edges[slot], grad)
                slots.append(slot)
    for at, slot in enumerate(slots):
        spot = block_of(cols, slot, own, r, size)
        total[spot, :] = total[spot, :] + terms[at]
    for k in range(n_row):

        def leave(i):
            rows = pl.ds(pl.multiple_of((k * own + i) * size, size), size)
            outs[k][pl.ds(pl.multiple_of(i * size, size), size), :] = total[rows, :].astype(BF16)

        each(own, leave)


def edge_body(n_row, n_col, size, depth, cols, count, place, *refs):
    grads, (held, out) = refs[:n_col], refs[n_col:]
    own = grads[0].shape[0] // size
    r, c, used = place[0], place[1], count[0]
    for offset in range(n_col):
        for i in range(own):
            row = (c ^ offset) * own + i
            grad = grads[offset][pl.ds(i * size, size), :]
            for k in range(depth):
                slot = k * n_col * own + row
                value = nt(grad, held[block_of(cols, slot, own, r, size), :])
                out[slot] = jnp.where(slot < used, value, jnp.zeros_like(value)).astype(BF16)


def activate(size, k, terms, base, grad_live, w_msg):
    rows = pl.ds(k * size, size)
    total = terms[0][rows, :].astype(F32)
    for term in terms[1:]:
        total = total + term[rows, :].astype(F32)
    high = total.astype(BF16)
    low = (total - high.astype(F32)).astype(BF16)
    pre = jnp.dot(high, w_msg[...], preferred_element_type=F32)
    pre = pre + jnp.dot(low, w_msg[...], preferred_element_type=F32) + base[rows, :]
    sig = jax.nn.sigmoid(pre)
    deriv = sig * (1.0 + pre * (1.0 - sig))
    return high, pre, sig, (grad_live[rows, :].astype(F32) * deriv).astype(BF16)


def act_body(size, n_terms, *refs):
    terms = refs[:n_terms]
    base, grad_live, w_msg, grad_w, grad_pre, summed = refs[n_terms:]
    for k in range(base.shape[0] // size):
        rows = pl.ds(k * size, size)
        high, _, _, grad = activate(size, k, terms, base, grad_live, w_msg)
        summed[rows, :] = high
        grad_pre[rows, :] = grad
        grad_w[rows, :] = nt(grad, w_msg[...]).astype(BF16)


def rest_body(size, n_terms, mask, *refs):
    terms = refs[:n_terms]
    base, grad_live, w_msg, w_self, hidden, own_part = refs[n_terms:]
    for k in range(base.shape[0] // size):
        rows = pl.ds(k * size, size)
        _, pre, sig, grad = activate(size, k, terms, base, grad_live, w_msg)
        value = (pre * sig).astype(BF16)
        picked = jnp.dot(select_rows(mask, k, size), value, preferred_element_type=F32)
        hidden[rows, :] = picked.astype(BF16)
        own_part[rows, :] = nt(grad, w_self[...])


def side_body(dims, n_edge, size, n_terms, n_rest, cols, count, place, *refs):
    edge_refs, rest_refs = refs[:n_edge], refs[n_edge : n_edge + n_rest]
    edge_grad, hidden, own_part = refs[n_edge + n_rest :]
    rest_body(size, n_terms, *rest_refs, hidden, own_part)
    edge_body(*dims, cols, count, place, *edge_refs, edge_grad)


def weight_body(factor, place, feats, grad_pre, summed, same, other, stack):
    width = feats.shape[1]
    grad = grad_pre[...]
    stack[pl.ds(0, width), :] = tn(summed[...], grad) * factor
    stack[pl.ds(width, width), :] = tn(feats[...], grad) * factor
    rest = stack.shape[0] - 2 * width
    total = jnp.sum(grad.astype(F32), axis=0, keepdims=True) * factor
    stack[pl.ds(2 * width, rest), :] = jnp.broadcast_to(total, (rest, width))
    half = stack.shape[0] // 2
    core = place[1] % 2
    same[...] = stack[pl.ds(pl.multiple_of(core * half, 8), half), :]
    other[...] = stack[pl.ds(pl.multiple_of((1 - core) * half, 8), half), :]


def join_body(place, same, other, w_msg, w_self, bias, stack):
    width = w_msg.shape[0]
    half = stack.shape[0] // 2
    core = place[1] % 2
    stack[pl.ds(pl.multiple_of(core * half, 8), half), :] = same[...]
    stack[pl.ds(pl.multiple_of((1 - core) * half, 8), half), :] = other[...]
    w_msg[...] = stack[pl.ds(0, width), :]
    w_self[...] = stack[pl.ds(width, width), :]
    bias[...] = stack[pl.ds(2 * width, 1), :]


def finish_body(size, mask, early, last, out):
    for k in range(mask.shape[0]):
        rows = pl.ds(k * size, size)
        picked = jnp.dot(select_rows(mask, k, size), last[rows, :], preferred_element_type=F32)
        out[rows, :] = (early[rows, :] + picked).astype(BF16)


def per_device(feats, w_msg, w_self, bias, hit_mask, block_cols, block_count, edge_vals, grad_out):
    n_row, n_col = lax.axis_size("row"), lax.axis_size("col")
    own_rows, width = feats.shape
    edges = edge_vals[0, 0]
    slots, size = edges.shape[0], edges.shape[1]
    own = own_rows // size
    tile_rows = n_col * own
    depth = slots // tile_rows
    cols, count = block_cols[0, 0], block_count[0]
    place = jnp.stack([lax.axis_index("row"), lax.axis_index("col")]).astype(jnp.int32)
    mask = hit_mask.reshape(own, size)
    block = jax.ShapeDtypeStruct((own_rows, width), BF16)
    wide = jax.ShapeDtypeStruct((own_rows, width), F32)
    edge_flops = 2 * slots * size * size * width
    dims = (n_row, n_col, size, depth)

    masked = kernel_call(
        functools.partial(mask_body, size),
        block,
        [HBM] * 2,
        VMEM,
        [
            pltpu.VMEM((own, size), jnp.int32),
            pltpu.VMEM((own_rows, width), BF16),
            pltpu.SemaphoreType.DMA((2,)),
        ],
        2 * own_rows * size * width,
        (mask, feats),
    )
    held, early = gather_rows(masked, "row")
    late_count, late_bias, _ = tie(count, bias, early)
    live = kernel_call(
        live_body,
        jax.ShapeDtypeStruct(edges.shape, BF16),
        [SMEM, VMEM],
        VMEM,
        [],
        0,
        (late_count, edges),
    )
    base, grad_live, w_here, feats_here = kernel_call(
        functools.partial(prepare_body, size),
        [wide, block, jax.ShapeDtypeStruct(w_msg.shape, BF16), block],
        [VMEM] * 6,
        [VMEM] * 4,
        [],
        2 * own_rows * width * (width + size),
        (mask, feats, w_msg, w_self, late_bias[None, :], grad_out),
    )

    *partial, together = kernel_call(
        functools.partial(spmm_body, *dims),
        [block] * n_col + [jax.ShapeDtypeStruct((n_row * own_rows, width), BF16)],
        [SMEM] * 2 + [VMEM] * (1 + n_row),
        [VMEM] * (n_col + 1),
        [],
        edge_flops,
        (cols, place, live, *held),
    )
    terms = scatter_by_offset(partial, "col")

    grad_w, grad_pre, summed = kernel_call(
        functools.partial(act_body, size, len(terms)),
        [block] * 3,
        [VMEM] * (len(terms) + 3),
        [VMEM] * 3,
        [],
        6 * own_rows * width * width,
        (*terms, base, grad_live, w_here),
    )
    grads = gather_by_offset(grad_w, "col")

    pieces = kernel_call(
        functools.partial(back_body, *dims),
        [block] * n_row,
        [SMEM] * 2 + [VMEM] * (1 + n_col),
        [VMEM] * n_row,
        [
            pltpu.VMEM((slots, size, width), F32),
            pltpu.VMEM((n_row * own_rows, width), F32),
        ],
        edge_flops,
        (cols, place, live, *grads),
    )

    rest = (mask, *terms, base, grad_live, w_here, w_self)
    edge_grad, hidden, own_part = kernel_call(
        functools.partial(side_body, dims, n_col + 1, size, len(terms), len(rest)),
        [jax.ShapeDtypeStruct((slots, size, size), BF16), block, wide],
        [SMEM] * 3 + [VMEM] * (n_col + 1 + len(rest)),
        [VMEM] * 3,
        [],
        edge_flops + 8 * own_rows * width * width,
        (cols, count, place, *grads, together, *rest),
    )

    rows = 2 * width + 32
    half = jax.ShapeDtypeStruct((rows // 2, width), F32)
    factor = 1.0 / math.sqrt(own_rows * n_row * n_col)
    same, other = kernel_call(
        functools.partial(weight_body, factor),
        [half, half],
        [SMEM] + [VMEM] * 3,
        [VMEM] * 2,
        [pltpu.VMEM((rows, width), F32)],
        4 * own_rows * width * width,
        (place, feats_here, grad_pre, summed),
    )
    *back, far = scatter_rows(pieces, "row")
    total = same + exchange(other, "col", 1)
    row_bits, col_bits = bits_of(n_row), bits_of(n_col)[1:]
    total = add_over(total, (row_bits.pop(min(1, len(row_bits) - 1)), 0))
    total, _ = tie(total, pieces[0])
    for bit in reversed(row_bits[1:]):
        total = add_over(total, (bit, 0))
    for bit in col_bits[:-1]:
        total = add_over(total, (0, bit))
    total, *_ = tie(total, far, own_part)
    total = add_over(total, (row_bits[0], 0), (0, col_bits[-1]))
    total, *_ = tie(total, own_part, *back[2:])
    square = jax.ShapeDtypeStruct((width, width), F32)
    msg_grad, self_grad, bias_grad = kernel_call(
        join_body,
        [square, square, jax.ShapeDtypeStruct((1, width), F32)],
        [SMEM] + [VMEM] * 2,
        [VMEM] * 3,
        [pltpu.VMEM((rows, width), F32)],
        0,
        (place, total, exchange(total, "col", 1)),
    )

    column = (hit_mask != 0)[:, None]
    early = jnp.where(column, sum(term.astype(F32) for term in back[:-1]), 0.0) + own_part
    early, last = tie(early, back[-1])
    grad_feats = kernel_call(
        functools.partial(finish_body, size),
        block,
        [VMEM] * 3,
        VMEM,
        [],
        2 * own_rows * size * width,
        (mask, early, last),
    )
    return hidden, grad_feats, edge_grad[None, None], msg_grad, self_grad, bias_grad[0]


def solution(mesh):
    placed = (
        P(("row", "col"), None),
        P(),
        P(),
        P(),
        P(("row", "col")),
        P("row", "col", None),
        P("row", "col"),
        P("row", "col", None, None, None),
        P(("row", "col"), None),
    )
    return jax.shard_map(
        per_device,
        mesh=mesh,
        in_specs=placed,
        out_specs=(
            P(("row", "col"), None),
            P(("row", "col"), None),
            P("row", "col", None, None, None),
            P(),
            P(),
            P(),
        ),
        check_vma=False,
    )
```
